32 devices in a mesh: dp: 16 (over z, y, x), tensor: 2 (over core).
Axes of the slice: x: 2, y: 2, z: 4, core: 2. Of those that a mesh axis runs over, the one named last changes fastest.
Arguments:
- tokens: bfloat16 [16384, 1408], P(('dp', 'tensor')), may hold values from -6 to 6
- ln1_gain: float32 [1408], replicated, may hold values from 0.1 to 1.9
- ln1_shift: float32 [1408], replicated, may hold values from -3 to 3
- w_qkv: bfloat16 [1408, 16, 264], P(None, 'tensor')
- w_out: bfloat16 [16, 88, 1408], P('tensor'), may hold values from -0.625 to 0.625
- ln2_gain: float32 [1408], replicated, may hold values from 0.1 to 1.9
- ln2_shift: float32 [1408], replicated, may hold values from -3 to 3
- w_proj: bfloat16 [5632, 3584], P('dp', 'tensor'), may hold values from -0.078125 to 0.078125
- proj_bias: float32 [3584], P('tensor'), may hold values from -3 to 3
- segments: int32 [16, 256], P('dp'), may hold values from 0 to 7, never falling along the last dimension, each value on 1 to 128 neighbouring positions
- owners: int32 [4096, 1], P('dp'), may hold values from 0 to 15; in each aligned block of 256 rows (0 to 255, 256 to 511, ...) at most 32 rows name the same one
Outputs:
- delivered: bfloat16 [8192, 3584], P('dp', 'tensor')
The draws below stay inside these ranges and needn't reach their ends.
Inputs may be any that keep to these rules, and one draw needn't show every extreme that they name: `segments`: within a pack numbers never fall, every image has 1 to 128 groups and one has exactly that many. `owners`: among the 256 merged tokens of one pack no owner gets more than 32; in some pack an owner gets exactly 32.
All inputs are finite; a program needn't handle non-finite values.
Results may differ from the reference program's by a relative error of at most 0.015.
Values may be sent and summed in bfloat16 or wider, within the bound.
A program may use at most 128 MiB of HBM per device.

```python
import math
import jax
import jax.numpy as jnp
import numpy as np
from jax import lax

D = 1408
HEADS = 16
HEAD = 88
OUT = 3584
PACK = 1024
IMGS = 8
G = 256
MERGED = 5632
CAP = 32
HGROUP = 8
TOKENS = 16384
N_DP = 16
N_TENSOR = 2


def draw_w_qkv(key, part):
    first_key = jax.random.fold_in(jax.random.fold_in(key, 11), 0)
    base = jax.random.normal(first_key, (D, HEADS, 3 * HEAD), jnp.float32) * D ** (-0.5)
    return base.astype(jnp.bfloat16)


def block_scale(own_key, shape, cuts, smallest, top_value):
    factor_of, own = 1.0, jax.random.fold_in(own_key, 6)
    for axis_at, parts in cuts:
        heights = jnp.exp(jax.random.uniform(jax.random.fold_in(own, axis_at), (parts,), jnp.float32, smallest / len(cuts), top_value / len(cuts)))
        factor_of = factor_of * jnp.repeat(heights, shape[axis_at] // parts).reshape([-1 if axis == axis_at else 1 for axis in range(len(shape))])
    return factor_of


def split_up(amount, total, limit, lean):
    weights = [(1 << 20) // math.isqrt(rank ** lean) + 1 for rank in range(2, amount + 1)]
    surplus, given = total - limit - (amount - 1), [1] * (amount - 1)
    while surplus > 0:
        candidates = [i for i in range(amount - 1) if given[i] < limit]
        mass, left = sum([weights[i] for i in candidates]), surplus
        for i in candidates:
            addition = min(limit - given[i], max(1, left * weights[i] // mass), surplus)
            given[i] = given[i] + addition
            surplus = surplus - addition
    return np.array([limit] + given)


def uneven_parts(rng, count, total, limit, lean):
    if count == 2:
        one = jax.random.randint(rng, (), max(1, total - limit), min(limit, total - 1) + 1)
        return jnp.stack([one, total - one])
    lengths = jnp.asarray(split_up(count, total, limit, lean), jnp.int32)
    pairs = (count - 1) // 2
    source_of, taker = lengths[1:1 + 2 * pairs:2], lengths[2:2 + 2 * pairs:2]
    slack = jnp.minimum(source_of - 1, limit - taker)
    shifted = jax.random.randint(jax.random.fold_in(rng, 1), (pairs,), 0, 1 << 20) % (slack + 1)
    lengths = lengths.at[1:1 + 2 * pairs:2].set(source_of - shifted).at[2:2 + 2 * pairs:2].set(taker + shifted)
    return lengths[jax.random.permutation(jax.random.fold_in(rng, 2), count)]


def assign_block(stream_key, own, number, rows, number_of, top, reach, skew):
    ranking = jax.random.permutation(stream_key, number_of)
    heavy_load, ordinary = shares(number_of, rows * top, reach, skew, True), shares(number_of, rows * top, reach, skew, False)
    places = jnp.arange(number_of)

    def named(sizes, rotation):
        used = int((sizes > 0).sum())
        fixed = max(1, used // 4)
        passed = fixed + (places - fixed + rotation * (used - fixed)) % max(1, number_of - fixed)
        return jnp.zeros((number_of,), jnp.int32).at[ranking[jnp.where(places < fixed, places, passed)]].set(jnp.asarray(sizes, jnp.int32))

    sizes = jnp.where(number % 4 == 0, named(heavy_load, number // 4), named(ordinary, number - number // 4 - 1))
    mixed = jax.random.permutation(jax.random.fold_in(own, 3), number_of)
    donor, receiver = mixed[0:number_of // 2 * 2:2], mixed[1:number_of // 2 * 2:2]
    slack = jnp.minimum(sizes[donor] - 1, reach - sizes[receiver]) // 2
    slack = jnp.where((donor == ranking[0]) | (receiver == ranking[0]) | (sizes[receiver] == 0), 0, jnp.maximum(slack, 0))
    passed = jax.random.randint(jax.random.fold_in(own, 4), (number_of // 2,), 0, 1 << 20) % (slack + 1)
    sizes = sizes.at[donor].add(-passed).at[receiver].add(passed)
    items = jnp.searchsorted(jnp.cumsum(sizes), jnp.arange(rows * top), side="right").astype(jnp.int32)
    table = items.reshape(top, rows).T
    table = table[jax.random.permutation(jax.random.fold_in(own, 1), rows)]
    rotation = jax.random.randint(jax.random.fold_in(own, 2), (rows, 1), 0, top)
    return jnp.take_along_axis(table, (jnp.arange(top)[None, :] + rotation) % top, axis=1)


def shares(number_of, total, reach, slope, full):
    portions = [(1 << 20) // math.isqrt(grade ** slope) + 1 for grade in range(1, number_of + 1)]
    largest = reach if full else min(reach, max(-(-total // number_of), total * portions[0] // sum(portions)))
    least = 1 if total - largest >= number_of - 1 else 0
    counts, spare = [largest] + [least] * (number_of - 1), total - largest - least * (number_of - 1)
    while spare > 0:
        movable = [i for i in range(1, number_of) if counts[i] < largest] or [i for i in range(1, number_of) if counts[i] < reach]
        pool, budget = sum([portions[i] for i in movable]), spare
        for i in movable:
            more = min(reach - counts[i], max(1, budget * portions[i] // pool), spare)
            counts[i] = counts[i] + more
            spare = spare - more
    return np.array(counts)


def gaussian(own_key, dims, scale, bound, cuts=(), kind=jnp.bfloat16):
    loudness = block_scale(own_key, dims, cuts, -0.22, 0.18) if cuts else 1.0
    entries = jax.random.normal(own_key, dims, jnp.float32) * scale * loudness
    return jnp.minimum(jnp.maximum(entries, -bound), bound).astype(kind)


def setup_inputs(seed: int = 0) -> dict:
    seeds = jax.random.split(jax.random.key(seed), 12)
    tokens = gaussian(seeds[0], (TOKENS, D), 1.0, 6.0, ((0, 32),))
    ln1_gain = jnp.clip(1.0 + 0.18 * jax.random.normal(seeds[1], (D,), jnp.float32), 0.1, 1.9)
    ln1_shift = gaussian(seeds[2], (D,), 0.3, 3.0, (), jnp.float32)
    w_qkv = draw_w_qkv(jax.random.fold_in(seeds[11], 71), 0)
    w_out = gaussian(seeds[4], (HEADS, HEAD, D), HEAD ** -0.5, 0.625, ((0, 2),))
    ln2_gain = jnp.clip(1.0 + 0.18 * jax.random.normal(seeds[5], (D,), jnp.float32), 0.1, 1.9)
    ln2_shift = gaussian(seeds[6], (D,), 0.3, 3.0, (), jnp.float32)
    w_proj = gaussian(seeds[7], (MERGED, OUT), MERGED ** -0.5, 0.078125, ((0, 16), (1, 2)))
    proj_bias = gaussian(seeds[8], (OUT,), 0.5, 3.0, ((0, 2),), jnp.float32)
    segments = jax.vmap(lambda own: jnp.searchsorted(jnp.cumsum(uneven_parts(own, IMGS, G, G // 2, 1)), jnp.arange(G), side="right"))(jax.random.split(seeds[9], N_DP)).reshape((N_DP, G)).astype(jnp.int32)
    owners_keys = jax.random.split(jax.random.fold_in(seeds[10], 1), (TOKENS // 4) // G)
    owners_turns = jax.random.permutation(jax.random.fold_in(seeds[10], 3), (TOKENS // 4) // G)
    owners = jax.vmap(lambda own, number: assign_block(jax.random.fold_in(seeds[10], 2), own, number, G, N_DP, 1, CAP, 2))(owners_keys, owners_turns).reshape((TOKENS // 4, 1))
    return dict(tokens=tokens, ln1_gain=ln1_gain, ln1_shift=ln1_shift, w_qkv=w_qkv, w_out=w_out, ln2_gain=ln2_gain, ln2_shift=ln2_shift, w_proj=w_proj, proj_bias=proj_bias, segments=segments, owners=owners)


def layer_norm(values, gain, shift):
    wide = values.astype(jnp.float32)
    average = lax.optimization_barrier(jnp.mean(wide, axis=-1, keepdims=True))
    centred = wide - average
    variance = lax.optimization_barrier(jnp.mean(centred * centred, axis=-1, keepdims=True))
    return centred * lax.rsqrt(variance + 1e-06) * gain + shift

def attend(heads_qkv, token_segs):
    row_count = heads_qkv.shape[0]
    width = heads_qkv.shape[2] // 3
    queries = heads_qkv[:, :, :width].astype(jnp.float32)
    keys_all = heads_qkv[:, :, width:2 * width].astype(jnp.float32)
    values_all = heads_qkv[:, :, 2 * width:].astype(jnp.float32)
    score_scale = 1.0 / jnp.sqrt(jnp.float32(width))
    block_rows = min(512, row_count)
    outputs = []
    for block_index in range(row_count // block_rows):
        lower = block_index * block_rows
        scores = jnp.einsum('qhd,khd->hqk', queries[lower:lower + block_rows], keys_all) * score_scale
        same = token_segs[lower:lower + block_rows][:, None] == token_segs[None, :]
        scores = jnp.where(same[None], scores, -jnp.inf)
        row_max = lax.optimization_barrier(jnp.max(scores, axis=-1, keepdims=True))
        exponent = jnp.exp(scores - row_max)
        probs = (exponent / lax.optimization_barrier(jnp.sum(exponent, axis=-1, keepdims=True))).astype(jnp.bfloat16)
        context = jnp.einsum('hqk,khd->qhd', probs.astype(jnp.float32), values_all)
        outputs.append(context.astype(jnp.bfloat16))
    return jnp.concatenate(outputs, axis=0)

def reference(tokens, ln1_gain, ln1_shift, w_qkv, w_out, ln2_gain, ln2_shift, w_proj, proj_bias, segments, owners):
    pack_tokens = tokens.reshape(N_DP, PACK, D)
    pack_owners = owners.reshape(N_DP, G)

    def one_pack(inputs):
        rows, segs, dests = inputs
        normed = layer_norm(rows, ln1_gain, ln1_shift).astype(jnp.bfloat16)
        heads_qkv = jnp.dot(normed, w_qkv.reshape(D, HEADS * 3 * HEAD), preferred_element_type=jnp.float32)
        heads_qkv = heads_qkv.astype(jnp.bfloat16).reshape(PACK, HEADS, 3 * HEAD)
        token_segs = jnp.repeat(segs, 4)
        context = attend(heads_qkv, token_segs)
        attn = jnp.zeros((PACK, D), jnp.float32)
        for group_index in range(N_TENSOR):
            lower = group_index * HGROUP
            term = jnp.dot(context[:, lower:lower + HGROUP].reshape(PACK, HGROUP * HEAD), w_out[lower:lower + HGROUP].reshape(HGROUP * HEAD, D), preferred_element_type=jnp.float32).astype(jnp.bfloat16)
            term = lax.optimization_barrier(term)
            attn = attn + term.astype(jnp.float32)
        hidden = (rows.astype(jnp.float32) + attn).astype(jnp.bfloat16)
        normed_two = layer_norm(hidden, ln2_gain, ln2_shift).astype(jnp.bfloat16)
        merged = normed_two.reshape(G, MERGED)
        projected = (jnp.dot(merged, w_proj, preferred_element_type=jnp.float32) + proj_bias).astype(jnp.bfloat16)
        onehot = (dests[:, None] == jnp.arange(N_DP, dtype=jnp.int32)[None, :]).astype(jnp.int32)
        earlier = jnp.cumsum(onehot, axis=0) - onehot
        position = lax.optimization_barrier(jnp.sum(earlier * onehot, axis=1)).astype(jnp.int32)
        return (projected, position)
    projected_all, positions = lax.map(one_pack, (pack_tokens, segments, pack_owners))
    pack_index = jnp.broadcast_to(jnp.arange(N_DP, dtype=jnp.int32)[:, None], (N_DP, G))
    delivered = jnp.zeros((N_DP, N_DP, CAP, OUT), jnp.bfloat16)
    delivered = delivered.at[pack_owners, pack_index, positions].set(projected_all)
    return delivered.reshape(N_DP * N_DP * CAP, OUT)
```

```python
import math

import jax
import jax.numpy as jnp
from jax import lax
from jax.experimental import pallas as pl
from jax.experimental.pallas import tpu as pltpu
from jax.sharding import PartitionSpec as P


def layer_norm(values, gain, shift):
    wide = values.astype(jnp.float32)
    average = jnp.mean(wide, axis=-1, keepdims=True)
    centred = wide - average
    variance = jnp.mean(centred * centred, axis=-1, keepdims=True)
    return centred * lax.rsqrt(variance + 1e-06) * gain + shift


def attend(heads_qkv, token_segs):
    row_count = heads_qkv.shape[0]
    width = heads_qkv.shape[2] // 3
    queries = heads_qkv[:, :, :width]
    keys_all = heads_qkv[:, :, width : 2 * width]
    values_all = heads_qkv[:, :, 2 * width :]
    score_scale = 1.0 / jnp.sqrt(jnp.float32(width))
    block_rows = min(512, row_count)
    outputs = []
    for block_index in range(row_count // block_rows):
        lower = block_index * block_rows
        scores = (
            jnp.einsum(
                "qhd,khd->hqk",
                queries[lower : lower + block_rows],
                keys_all,
                preferred_element_type=jnp.float32,
            )
            * score_scale
        )
        same = token_segs[lower : lower + block_rows][:, None] == token_segs[None, :]
        scores = jnp.where(same[None], scores, -jnp.inf)
        row_max = jnp.max(scores, axis=-1, keepdims=True)
        exponent = jnp.exp(scores - row_max)
        probs = (exponent / jnp.sum(exponent, axis=-1, keepdims=True)).astype(jnp.bfloat16)
        context = jnp.einsum("hqk,khd->qhd", probs, values_all, preferred_element_type=jnp.float32)
        outputs.append(context.astype(jnp.bfloat16))
    return jnp.concatenate(outputs, axis=0)


def shards(
    tokens,
    ln1_gain,
    ln1_shift,
    w_qkv,
    w_out,
    ln2_gain,
    ln2_shift,
    w_proj,
    proj_bias,
    segments,
    owners,
):
    dp_count = lax.axis_size("dp")
    gathered = lax.all_gather(tokens, "tensor", axis=0, tiled=True)
    row_count = gathered.shape[0]
    normed = layer_norm(gathered, ln1_gain, ln1_shift).astype(jnp.bfloat16)
    heads_here = w_qkv.shape[1]
    heads_qkv = jnp.dot(
        normed, w_qkv.reshape(w_qkv.shape[0], -1), preferred_element_type=jnp.float32
    )
    heads_qkv = heads_qkv.astype(jnp.bfloat16).reshape(row_count, heads_here, -1)
    token_segs = jnp.repeat(segments[0], 4)
    context = attend(heads_qkv, token_segs).reshape(row_count, -1)
    out_flat = w_out.reshape(-1, w_out.shape[2])
    attn_all = lax.psum(
        jnp.dot(context, out_flat, preferred_element_type=jnp.float32).astype(jnp.bfloat16),
        "tensor",
    ).astype(jnp.float32)
    hidden = (gathered.astype(jnp.float32) + attn_all).astype(jnp.bfloat16)
    normed_all = layer_norm(hidden, ln2_gain, ln2_shift).astype(jnp.bfloat16)
    groups = row_count // 4
    merged = normed_all.reshape(groups, -1)
    summed = jnp.dot(
        merged, lax.all_gather(w_proj, "dp", axis=0, tiled=True), preferred_element_type=jnp.float32
    )
    projected = (summed + proj_bias).astype(jnp.bfloat16)
    dests = owners[:, 0]
    onehot = (dests[:, None] == jnp.arange(dp_count, dtype=jnp.int32)[None, :]).astype(jnp.int32)
    earlier = jnp.cumsum(onehot, axis=0) - onehot
    position = jnp.sum(earlier * onehot, axis=1)
    capacity = 2 * groups // dp_count
    slot_index = dests * capacity + position
    scatter_table = (
        slot_index[None, :] == jnp.arange(dp_count * capacity, dtype=jnp.int32)[:, None]
    ).astype(jnp.bfloat16)
    outgoing = jnp.dot(scatter_table, projected, preferred_element_type=jnp.float32).astype(
        jnp.bfloat16
    )
    outgoing = outgoing.reshape(dp_count, capacity, -1)
    arrived = lax.all_to_all(outgoing, "dp", split_axis=0, concat_axis=0, tiled=True)
    return arrived.reshape(dp_count * capacity, -1)


def norm_rows(wide, gain, shift):
    average = jnp.mean(wide, axis=-1, keepdims=True)
    centred = wide - average
    variance = jnp.mean(centred * centred, axis=-1, keepdims=True)
    return centred * lax.rsqrt(variance + 1e-06) * gain + shift


def attention_kernel(
    own_ref,
    peer_ref,
    gain_ref,
    shift_ref,
    w_ref,
    segs_col_ref,
    segs_row_ref,
    w_out_ref,
    own_term_ref,
    peer_term_ref,
    normed_ref,
    context_ref,
):
    head = pl.program_id(0)
    half = own_ref.shape[0]
    rows = 2 * half
    width = w_ref.shape[0] // 3
    score_scale = 1.0 / math.sqrt(width)
    step_rows = 128

    @pl.when(head == 0)
    def _():
        for part, source in enumerate((own_ref, peer_ref)):

            @pl.loop(0, half // step_rows)
            def _(step):
                at = pl.multiple_of(step * step_rows, step_rows)
                wide = source[pl.ds(at, step_rows), :].astype(jnp.float32)
                normed = norm_rows(wide, gain_ref[...], shift_ref[...])
                to = pl.multiple_of(part * half + step * step_rows, step_rows)
                normed_ref[pl.ds(to, step_rows), :] = normed.astype(jnp.bfloat16)

    qkv = lax.dot_general(
        w_ref[...], normed_ref[...], (((1,), (1,)), ((), ())), preferred_element_type=jnp.float32
    )
    queries = qkv[:width].astype(jnp.bfloat16)
    keys = qkv[width : 2 * width].T.astype(jnp.bfloat16)
    values = qkv[2 * width :].astype(jnp.bfloat16)
    chunk = 256
    for index in range(rows // chunk):
        lanes = slice(index * chunk, (index + 1) * chunk)
        scores = jnp.dot(keys, queries[:, lanes], preferred_element_type=jnp.float32) * score_scale
        same = segs_col_ref[...] == segs_row_ref[:, lanes]
        scores = jnp.where(same, scores, -jnp.inf)
        exponent = jnp.exp(scores - jnp.max(scores, axis=0, keepdims=True))
        total = jnp.sum(exponent, axis=0, keepdims=True)
        summed = jnp.dot(values, exponent.astype(jnp.bfloat16), preferred_element_type=jnp.float32)
        context_ref[pl.ds(pl.multiple_of(head * width, 8), width), lanes] = summed / total

    @pl.when(head == pl.num_programs(0) - 1)
    def _():
        for index in range(rows // chunk):
            lanes = slice(index * chunk, (index + 1) * chunk)
            context = context_ref[:, lanes].T.astype(jnp.bfloat16)
            term = jnp.dot(context, w_out_ref[...], preferred_element_type=jnp.float32)
            target = own_term_ref if index * chunk < half else peer_term_ref
            at = index * chunk % half
            target[at : at + chunk, :] = term.astype(jnp.bfloat16)


def attention_terms(own, peer, gain, shift, w_heads, segs, w_out):
    half, depth = own.shape
    heads, columns, _ = w_heads.shape
    rows = 2 * half
    whole = lambda *shape: pl.BlockSpec(shape, lambda head: (0,) * len(shape))
    term = jax.ShapeDtypeStruct((half, depth), jnp.bfloat16)
    return pl.pallas_call(
        attention_kernel,
        grid=(heads,),
        in_specs=[
            whole(half, depth),
            whole(half, depth),
            whole(1, depth),
            whole(1, depth),
            pl.BlockSpec((None, columns, depth), lambda head: (head, 0, 0)),
            whole(rows, 1),
            whole(1, rows),
            whole(*w_out.shape),
        ],
        out_specs=[whole(half, depth), whole(half, depth)],
        out_shape=[term, term],
        scratch_shapes=[
            pltpu.VMEM((rows, depth), jnp.bfloat16),
            pltpu.VMEM((w_out.shape[0], rows), jnp.float32),
        ],
        compiler_params=pltpu.CompilerParams(vmem_limit_bytes=50 * 2**20),
        cost_estimate=pl.CostEstimate(flops=10**9, bytes_accessed=10**6, transcendentals=0),
    )(own, peer, gain[None], shift[None], w_heads, segs[:, None], segs[None], w_out)


def merge_kernel(tokens_ref, here_ref, there_ref, gain_ref, shift_ref, merged_ref, normed_ref):
    depth = tokens_ref.shape[1]
    step_rows = 128

    @pl.loop(0, tokens_ref.shape[0] // step_rows)
    def _(step):
        at = pl.ds(pl.multiple_of(step * step_rows, step_rows), step_rows)
        attn = here_ref[at, :].astype(jnp.float32) + there_ref[at, :].astype(jnp.float32)
        hidden = (tokens_ref[at, :].astype(jnp.float32) + attn).astype(jnp.bfloat16)
        normed = norm_rows(hidden.astype(jnp.float32), gain_ref[...], shift_ref[...])
        for piece in range(depth // 128):
            normed_ref[piece] = normed[:, piece * 128 : (piece + 1) * 128]
        to = pl.ds(pl.multiple_of(step * (step_rows // 4), step_rows // 4), step_rows // 4)
        for place in range(4):
            for piece in range(depth // 128):
                picked = normed_ref[piece, pl.ds(place, step_rows // 4, stride=4), :]
                lower = place * depth + piece * 128
                merged_ref[to, lower : lower + 128] = picked.astype(jnp.bfloat16)


def merge_tokens(tokens, here, there, gain, shift):
    rows, depth = tokens.shape
    return pl.pallas_call(
        merge_kernel,
        out_shape=jax.ShapeDtypeStruct((rows // 4, 4 * depth), jnp.bfloat16),
        scratch_shapes=[pltpu.VMEM((depth // 128, 128, 128), jnp.float32)],
        compiler_params=pltpu.CompilerParams(vmem_limit_bytes=32 * 2**20),
        cost_estimate=pl.CostEstimate(flops=10**7, bytes_accessed=10**6, transcendentals=0),
    )(tokens, here, there, gain[None], shift[None])


def project_kernel(a_ref, b_ref, c_ref, d_ref, w_ref, bias_ref, slots_ref, side_ref, out_ref, total_ref):
    step = pl.program_id(0)
    rows = a_ref.shape[0]

    @pl.when(step == 0)
    def _():
        total_ref[...] = jnp.zeros_like(total_ref)

    for index, block in enumerate((a_ref, b_ref, c_ref, d_ref)):
        total_ref[index * rows : (index + 1) * rows, :] += jnp.dot(
            block[...], w_ref[...], preferred_element_type=jnp.float32
        )

    @pl.when(step == pl.num_programs(0) - 1)
    def _():
        owners_count, _, capacity, columns = out_ref.shape
        places = lax.broadcasted_iota(jnp.int32, (owners_count * capacity, 2 * rows), 0)
        for pack in range(2):
            projected = total_ref[2 * pack * rows : 2 * (pack + 1) * rows, :] + bias_ref[...]
            table = (places == slots_ref[pack : pack + 1, :]).astype(jnp.bfloat16)
            placed = jnp.dot(
                table, projected.astype(jnp.bfloat16), preferred_element_type=jnp.float32
            ).astype(jnp.bfloat16)
            out_ref[:, jnp.bitwise_xor(side_ref[0], pack)] = placed.reshape(owners_count, capacity, columns)


def project_blocks(blocks, weights, bias, slots, side, owners_count, capacity):
    rows, depth = blocks[0].shape
    columns = weights.shape[1]
    step_depth = depth // 4
    shape = (owners_count, 2, capacity, columns)
    block = pl.BlockSpec((rows, step_depth), lambda step: (0, step))
    return pl.pallas_call(
        project_kernel,
        grid=(4,),
        in_specs=[block] * 4
        + [
            pl.BlockSpec((step_depth, columns), lambda step: (step, 0)),
            pl.BlockSpec((1, columns), lambda step: (0, 0)),
            pl.BlockSpec(slots.shape, lambda step: (0, 0)),
            pl.BlockSpec(memory_space=pltpu.SMEM),
        ],
        out_specs=pl.BlockSpec(shape, lambda step: (0, 0, 0, 0)),
        out_shape=jax.ShapeDtypeStruct(shape, jnp.bfloat16),
        scratch_shapes=[pltpu.VMEM((4 * rows, columns), jnp.float32)],
        compiler_params=pltpu.CompilerParams(vmem_limit_bytes=40 * 2**20),
        cost_estimate=pl.CostEstimate(flops=10**9, bytes_accessed=10**7, transcendentals=0),
    )(*blocks, weights, bias, slots, side[None])


def slot_numbers(dests, dp_count, capacity):
    onehot = (dests[:, None] == jnp.arange(dp_count, dtype=jnp.int32)[None, :]).astype(jnp.int32)
    earlier = jnp.cumsum(onehot, axis=0) - onehot
    return dests * capacity + jnp.sum(earlier * onehot, axis=1)


def paired_shards(
    tokens,
    ln1_gain,
    ln1_shift,
    w_qkv,
    w_out,
    ln2_gain,
    ln2_shift,
    w_proj,
    proj_bias,
    segments,
    owners,
):
    dp_count = lax.axis_size("dp")
    core = lax.axis_index("tensor")
    side = lax.axis_index("dp") % 2
    swap_cores = lambda array: lax.ppermute(array, "tensor", [(0, 1), (1, 0)])
    swap_chips = lambda array: lax.ppermute(array, "dp", [(i, i ^ 1) for i in range(dp_count)])
    columns = w_proj.shape[1] // 2
    kept = lax.dynamic_slice_in_dim(w_proj, side * columns, columns, axis=1)
    given = lax.dynamic_slice_in_dim(w_proj, (1 - side) * columns, columns, axis=1)
    taken = swap_chips(given)
    pair_rows = jnp.where(
        side == 0,
        jnp.concatenate([kept, taken], axis=0),
        jnp.concatenate([taken, kept], axis=0),
    )
    groups_of_side = [list(range(0, dp_count, 2)), list(range(1, dp_count, 2))]
    weights = lax.all_gather(
        pair_rows, "dp", axis=0, tiled=True, axis_index_groups=groups_of_side
    )
    bias = lax.dynamic_slice_in_dim(proj_bias, side * columns, columns)[None]

    other = swap_cores(tokens)
    half = tokens.shape[0]
    groups = 2 * half // 4
    token_segs = jnp.repeat(jnp.roll(segments[0], -core * (groups // 2)), 4)
    capacity = 2 * groups // dp_count
    slots = jnp.roll(slot_numbers(owners[:, 0], dp_count, capacity), -core * (groups // 2))
    slots = jnp.stack([slots, swap_chips(slots)])

    here, there = attention_terms(
        tokens,
        other,
        ln1_gain,
        ln1_shift,
        w_qkv.transpose(1, 2, 0),
        token_segs,
        w_out.reshape(-1, w_out.shape[2]),
    )
    merged = merge_tokens(tokens, here, swap_cores(there), ln2_gain, ln2_shift)
    far = swap_chips(merged)
    blocks = (merged, swap_cores(merged), far, swap_cores(far))
    outgoing = project_blocks(blocks, weights, bias, slots, side, dp_count, capacity)
    arrived = lax.all_to_all(outgoing, "dp", split_axis=0, concat_axis=0, tiled=True)
    arrived = arrived.reshape(dp_count // 2, 2, 2, capacity, columns).transpose(0, 2, 3, 1, 4)
    return arrived.reshape(dp_count * capacity, 2 * columns)


def solution(mesh):
    paired = mesh.shape["tensor"] == 2 and mesh.shape["dp"] == 16
    return jax.shard_map(
        paired_shards if paired else shards,
        mesh=mesh,
        in_specs=(
            P(("dp", "tensor"), None),
            P(),
            P(),
            P(None, "tensor", None),
            P("tensor", None, None),
            P(),
            P(),
            P("dp", "tensor"),
            P("tensor"),
            P("dp", None),
            P("dp", None),
        ),
        out_specs=P("dp", "tensor"),
        check_vma=False,
    )
```

```python
import math

import jax
import jax.numpy as jnp
from jax import lax
from jax.experimental import pallas as pl
from jax.experimental.pallas import tpu as pltpu
from jax.sharding import PartitionSpec as P


def layer_norm(values, gain, shift):
    wide = values.astype(jnp.float32)
    average = jnp.mean(wide, axis=-1, keepdims=True)
    centred = wide - average
    variance = jnp.mean(centred * centred, axis=-1, keepdims=True)
    return centred * lax.rsqrt(variance + 1e-06) * gain + shift


def attend(heads_qkv, token_segs):
    row_count = heads_qkv.shape[0]
    width = heads_qkv.shape[2] // 3
    queries = heads_qkv[:, :, :width]
    keys_all = heads_qkv[:, :, width : 2 * width]
    values_all = heads_qkv[:, :, 2 * width :]
    score_scale = 1.0 / jnp.sqrt(jnp.float32(width))
    block_rows = min(512, row_count)
    outputs = []
    for block_index in range(row_count // block_rows):
        lower = block_index * block_rows
        scores = (
            jnp.einsum(
                "qhd,khd->hqk",
                queries[lower : lower + block_rows],
                keys_all,
                preferred_element_type=jnp.float32,
            )
            * score_scale
        )
        same = token_segs[lower : lower + block_rows][:, None] == token_segs[None, :]
        scores = jnp.where(same[None], scores, -jnp.inf)
        row_max = jnp.max(scores, axis=-1, keepdims=True)
        exponent = jnp.exp(scores - row_max)
        probs = (exponent / jnp.sum(exponent, axis=-1, keepdims=True)).astype(jnp.bfloat16)
        context = jnp.einsum("hqk,khd->qhd", probs, values_all, preferred_element_type=jnp.float32)
        outputs.append(context.astype(jnp.bfloat16))
    return jnp.concatenate(outputs, axis=0)


def shards(
    tokens,
    ln1_gain,
    ln1_shift,
    w_qkv,
    w_out,
    ln2_gain,
    ln2_shift,
    w_proj,
    proj_bias,
    segments,
    owners,
):
    dp_count = lax.axis_size("dp")
    gathered = lax.all_gather(tokens, "tensor", axis=0, tiled=True)
    row_count = gathered.shape[0]
    normed = layer_norm(gathered, ln1_gain, ln1_shift).astype(jnp.bfloat16)
    heads_here = w_qkv.shape[1]
    heads_qkv = jnp.dot(
        normed, w_qkv.reshape(w_qkv.shape[0], -1), preferred_element_type=jnp.float32
    )
    heads_qkv = heads_qkv.astype(jnp.bfloat16).reshape(row_count, heads_here, -1)
    token_segs = jnp.repeat(segments[0], 4)
    context = attend(heads_qkv, token_segs).reshape(row_count, -1)
    out_flat = w_out.reshape(-1, w_out.shape[2])
    attn_all = lax.psum(
        jnp.dot(context, out_flat, preferred_element_type=jnp.float32).astype(jnp.bfloat16),
        "tensor",
    ).astype(jnp.float32)
    hidden = (gathered.astype(jnp.float32) + attn_all).astype(jnp.bfloat16)
    normed_all = layer_norm(hidden, ln2_gain, ln2_shift).astype(jnp.bfloat16)
    groups = row_count // 4
    merged = normed_all.reshape(groups, -1)
    summed = jnp.dot(
        merged, lax.all_gather(w_proj, "dp", axis=0, tiled=True), preferred_element_type=jnp.float32
    )
    projected = (summed + proj_bias).astype(jnp.bfloat16)
    dests = owners[:, 0]
    onehot = (dests[:, None] == jnp.arange(dp_count, dtype=jnp.int32)[None, :]).astype(jnp.int32)
    earlier = jnp.cumsum(onehot, axis=0) - onehot
    position = jnp.sum(earlier * onehot, axis=1)
    capacity = 2 * groups // dp_count
    slot_index = dests * capacity + position
    scatter_table = (
        slot_index[None, :] == jnp.arange(dp_count * capacity, dtype=jnp.int32)[:, None]
    ).astype(jnp.bfloat16)
    outgoing = jnp.dot(scatter_table, projected, preferred_element_type=jnp.float32).astype(
        jnp.bfloat16
    )
    outgoing = outgoing.reshape(dp_count, capacity, -1)
    arrived = lax.all_to_all(outgoing, "dp", split_axis=0, concat_axis=0, tiled=True)
    return arrived.reshape(dp_count * capacity, -1)


def norm_rows(wide, gain, shift):
    average = jnp.mean(wide, axis=-1, keepdims=True)
    centred = wide - average
    variance = jnp.mean(centred * centred, axis=-1, keepdims=True)
    return centred * lax.rsqrt(variance + 1e-06) * gain + shift


MESH = pl.DeviceIdType.MESH
FIRST_SENDS = ((0, 4), (0, 1), (0, 2), (0, 8))
AFTER_PAIR = ((4, 8), (4, 2), (4, 1))
AFTER_NEAR = ((1, 2), (8, 1), (8, 2))
ALL_SENDS = FIRST_SENDS + AFTER_PAIR + AFTER_NEAR + ((6, 1), (12, 2), (12, 1), (9, 2), (14, 1))


def flipped(index, offset):
    result = index
    for bit in range(4):
        if offset >> bit & 1:
            result = result + (1 << bit) * (1 - 2 * (index // (1 << bit) % 2))
    return result


def sublayer_kernel(
    own_ref,
    gain1_ref,
    shift1_ref,
    w_ref,
    segs_col_ref,
    segs_row_ref,
    w_out_ref,
    gain2_ref,
    shift2_ref,
    w_proj_ref,
    bias_ref,
    slots_ref,
    out_ref,
    peer_ref,
    normed_ref,
    context_ref,
    here_ref,
    there_ref,
    arrived_ref,
    pieces_ref,
    blocks_ref,
    gathered_ref,
    total_ref,
    far_slots_ref,
    send_sems,
    recv_sems,
):
    dp, core = lax.axis_index("dp"), lax.axis_index("tensor")
    half, depth = own_ref.shape
    rows = 2 * half
    width = w_ref.shape[1] // 3
    columns = gathered_ref.shape[2]
    score_scale = 1.0 / math.sqrt(width)
    parity = dp // 4 % 2
    beside = (dp, 1 - core)
    facing = (flipped(dp, 4), core)

    def remote(source, target, number, device):
        return pltpu.make_async_remote_copy(
            src_ref=source,
            dst_ref=target,
            send_sem=send_sems.at[number],
            recv_sem=recv_sems.at[number],
            device_id=device,
            device_id_type=MESH,
        )

    def lanes_of(side):
        return pl.ds(pl.multiple_of(side * columns, 128), columns)

    def shard_copy(shard, partner):
        index = flipped(dp, shard)
        if shard == 0:
            side = 1 - parity if partner == 4 else parity
            source = w_proj_ref.at[:, lanes_of(side)]
        else:
            source = gathered_ref.at[index]
        return remote(source, gathered_ref.at[index], shard ^ partner, (flipped(dp, partner), core))

    def wait_shard(offset):
        place = gathered_ref.at[flipped(dp, offset)]
        remote(place, place, offset, facing).wait_recv()

    barrier = pltpu.get_barrier_semaphore()
    for device in [(flipped(dp, bit), core) for bit in (1, 2, 4, 8)] + [beside]:
        pl.semaphore_signal(barrier, inc=1, device_id=device, device_id_type=MESH)
    pl.semaphore_wait(barrier, 5)

    token_copy = remote(own_ref, peer_ref, 16, beside)
    token_copy.start()
    for send in FIRST_SENDS:
        shard_copy(*send).start()
    slots_copy = remote(slots_ref, far_slots_ref, 21, facing)
    slots_copy.start()
    own_copy = pltpu.make_async_copy(
        w_proj_ref.at[:, lanes_of(parity)], gathered_ref.at[dp], recv_sems.at[0]
    )
    own_copy.start()

    step_rows = 128

    def first_norm(part, source):
        @pl.loop(0, half // step_rows)
        def _(step):
            at = pl.multiple_of(step * step_rows, step_rows)
            wide = source[pl.ds(at, step_rows), :].astype(jnp.float32)
            normed = norm_rows(wide, gain1_ref[...], shift1_ref[...])
            to = pl.multiple_of(part * half + step * step_rows, step_rows)
            normed_ref[pl.ds(to, step_rows), :] = normed.astype(jnp.bfloat16)

    first_norm(0, own_ref)
    token_copy.wait_recv()
    first_norm(1, peer_ref)

    chunk = 256

    def heads(first, last):
        @pl.loop(first, last)
        def _(head):
            qkv = lax.dot_general(
                w_ref[head],
                normed_ref[...],
                (((1,), (1,)), ((), ())),
                preferred_element_type=jnp.float32,
            )
            queries = qkv[:width].astype(jnp.bfloat16)
            keys = qkv[width : 2 * width].T.astype(jnp.bfloat16)
            values = qkv[2 * width :].astype(jnp.bfloat16)
            for index in range(rows // chunk):
                lanes = slice(index * chunk, (index + 1) * chunk)
                scores = jnp.dot(keys, queries[:, lanes], preferred_element_type=jnp.float32)
                same = segs_col_ref[...] == segs_row_ref[:, lanes]
                scores = jnp.where(same, scores * score_scale, -jnp.inf)
                exponent = jnp.exp(scores - jnp.max(scores, axis=0, keepdims=True))
                total = jnp.sum(exponent, axis=0, keepdims=True)
                summed = jnp.dot(
                    values, exponent.astype(jnp.bfloat16), preferred_element_type=jnp.float32
                )
                context_ref[head, :, lanes] = summed / total

    heads(0, 3)
    wait_shard(4)
    for send in AFTER_PAIR:
        shard_copy(*send).start()
    heads(3, 6)
    wait_shard(1)
    wait_shard(8)
    for send in AFTER_NEAR:
        shard_copy(*send).start()
    heads(6, w_ref.shape[0])
    wait_shard(6)
    shard_copy(6, 1).start()

    def terms(first, target):
        for index in range(half // chunk):
            lanes = slice(first + index * chunk, first + (index + 1) * chunk)
            context = context_ref[:, :, lanes].reshape(-1, chunk).T.astype(jnp.bfloat16)
            term = jnp.dot(context, w_out_ref[...], preferred_element_type=jnp.float32)
            target[index * chunk : (index + 1) * chunk, :] = term.astype(jnp.bfloat16)

    terms(half, there_ref)
    term_copy = remote(there_ref, arrived_ref, 17, beside)
    term_copy.start()
    terms(0, here_ref)
    term_copy.wait_recv()

    @pl.loop(0, half // step_rows)
    def _(step):
        at = pl.ds(pl.multiple_of(step * step_rows, step_rows), step_rows)
        attn = here_ref[at, :].astype(jnp.float32) + arrived_ref[at, :].astype(jnp.float32)
        hidden = (own_ref[at, :].astype(jnp.float32) + attn).astype(jnp.bfloat16)
        normed = norm_rows(hidden.astype(jnp.float32), gain2_ref[...], shift2_ref[...])
        for piece in range(depth // 128):
            pieces_ref[piece] = normed[:, piece * 128 : (piece + 1) * 128]
        quarter = step_rows // 4
        to = pl.ds(pl.multiple_of(step * quarter, quarter), quarter)
        for place in range(4):
            for piece in range(depth // 128):
                picked = pieces_ref[piece, pl.ds(place, quarter, stride=4), :]
                lanes = slice(piece * 128, (piece + 1) * 128)
                blocks_ref[0, place, to, lanes] = picked.astype(jnp.bfloat16)

    far_copy = remote(blocks_ref.at[0], blocks_ref.at[2], 18, facing)
    far_copy.start()
    near_copy = remote(blocks_ref.at[0], blocks_ref.at[1], 19, beside)
    near_copy.start()

    block_rows = blocks_ref.shape[2]

    def project(offset, first, fresh):
        place = flipped(dp, offset) // 4
        weights = gathered_ref[pl.ds(4 * place, 4)].reshape(-1, columns)
        for block in (first, first + 1):
            at = slice(block * block_rows, (block + 1) * block_rows)
            product = jnp.dot(blocks_ref[block, place], weights, preferred_element_type=jnp.float32)
            total_ref[at, :] = product if fresh else total_ref[at, :] + product

    wait_shard(12)
    shard_copy(12, 2).start()
    shard_copy(12, 1).start()
    wait_shard(9)
    shard_copy(9, 2).start()
    near_copy.wait_recv()
    own_copy.wait()
    wait_shard(2)
    wait_shard(3)
    project(0, 0, True)
    wait_shard(14)
    shard_copy(14, 1).start()
    far_copy.wait_recv()
    across_copy = remote(blocks_ref.at[2], blocks_ref.at[3], 20, beside)
    across_copy.start()
    wait_shard(5)
    wait_shard(7)
    project(4, 0, False)
    across_copy.wait_recv()
    project(0, 2, True)
    project(4, 2, False)
    wait_shard(10)
    wait_shard(11)
    project(8, 0, False)
    project(8, 2, False)
    wait_shard(13)
    wait_shard(15)
    project(12, 0, False)
    project(12, 2, False)
    slots_copy.wait_recv()

    dp_count, _, capacity, _ = out_ref.shape
    places = lax.broadcasted_iota(jnp.int32, (dp_count * capacity, 2 * block_rows), 0)
    for pack, slots in enumerate((slots_ref, far_slots_ref)):
        at = slice(2 * pack * block_rows, 2 * (pack + 1) * block_rows)
        projected = (total_ref[at, :] + bias_ref[...]).astype(jnp.bfloat16)
        table = (places == slots[...]).astype(jnp.bfloat16)
        placed = jnp.dot(table, projected, preferred_element_type=jnp.float32)
        slot = parity if pack == 0 else 1 - parity
        out_ref[:, slot] = placed.astype(jnp.bfloat16).reshape(dp_count, capacity, columns)

    for send in ALL_SENDS:
        shard_copy(*send).wait_send()
    for copy in (token_copy, slots_copy, term_copy, far_copy, near_copy, across_copy):
        copy.wait_send()


def slot_numbers(dests, dp_count, capacity):
    onehot = (dests[:, None] == jnp.arange(dp_count, dtype=jnp.int32)[None, :]).astype(jnp.int32)
    earlier = jnp.cumsum(onehot, axis=0) - onehot
    return dests * capacity + jnp.sum(earlier * onehot, axis=1)


def paired_shards(
    tokens,
    ln1_gain,
    ln1_shift,
    w_qkv,
    w_out,
    ln2_gain,
    ln2_shift,
    w_proj,
    proj_bias,
    segments,
    owners,
):
    dp_count = lax.axis_size("dp")
    core = lax.axis_index("tensor")
    parity = lax.axis_index("dp") // 4 % 2
    columns = w_proj.shape[1] // 2
    half, depth = tokens.shape
    groups = 2 * half // 4
    capacity = 2 * groups // dp_count
    bias = lax.dynamic_slice_in_dim(proj_bias, parity * columns, columns)
    token_segs = jnp.repeat(jnp.roll(segments[0], -core * (groups // 2)), 4)
    slots = jnp.roll(slot_numbers(owners[:, 0], dp_count, capacity), -core * (groups // 2))
    heads_here, width, _ = w_out.shape
    half_rows = pltpu.VMEM((half, depth), jnp.bfloat16)
    outgoing = pl.pallas_call(
        sublayer_kernel,
        in_specs=[pl.BlockSpec(memory_space=pltpu.VMEM)] * 12,
        out_specs=pl.BlockSpec(memory_space=pltpu.VMEM),
        out_shape=jax.ShapeDtypeStruct((dp_count, 2, capacity, columns), jnp.bfloat16),
        scratch_shapes=[
            half_rows,
            pltpu.VMEM((2 * half, depth), jnp.bfloat16),
            pltpu.VMEM((heads_here, width, 2 * half), jnp.float32),
            half_rows,
            half_rows,
            half_rows,
            pltpu.VMEM((depth // 128, 128, 128), jnp.float32),
            pltpu.VMEM((4, 4, half // 4, depth), jnp.bfloat16),
            pltpu.VMEM((dp_count, w_proj.shape[0], columns), jnp.bfloat16),
            pltpu.VMEM((half, columns), jnp.float32),
            pltpu.VMEM((1, groups), jnp.int32),
            pltpu.SemaphoreType.DMA((22,)),
            pltpu.SemaphoreType.DMA((22,)),
        ],
        compiler_params=pltpu.CompilerParams(
            collective_id=0, has_side_effects=True, vmem_limit_bytes=60 * 2**20
        ),
        cost_estimate=pl.CostEstimate(flops=10**10, bytes_accessed=10**7, transcendentals=0),
    )(
        tokens,
        ln1_gain[None],
        ln1_shift[None],
        w_qkv.transpose(1, 2, 0),
        token_segs[:, None],
        token_segs[None],
        w_out.reshape(-1, depth),
        ln2_gain[None],
        ln2_shift[None],
        w_proj,
        bias[None],
        slots[None],
    )
    arrived = lax.all_to_all(outgoing, "dp", split_axis=0, concat_axis=0, tiled=True)
    arrived = arrived.reshape(dp_count // 8, 2, 4, 2, capacity, columns)
    return arrived.transpose(0, 3, 2, 4, 1, 5).reshape(dp_count * capacity, 2 * columns)


def solution(mesh):
    paired = mesh.shape["tensor"] == 2 and mesh.shape["dp"] == 16
    return jax.shard_map(
        paired_shards if paired else shards,
        mesh=mesh,
        in_specs=(
            P(("dp", "tensor"), None),
            P(),
            P(),
            P(None, "tensor", None),
            P("tensor", None, None),
            P(),
            P(),
            P("dp", "tensor"),
            P("tensor"),
            P("dp", None),
            P("dp", None),
        ),
        out_specs=P("dp", "tensor"),
        check_vma=False,
    )
```

```python
import math

import jax
import jax.numpy as jnp
from jax import lax
from jax.experimental import pallas as pl
from jax.experimental.pallas import tpu as pltpu
from jax.sharding import PartitionSpec as P


def layer_norm(values, gain, shift):
    wide = values.astype(jnp.float32)
    average = jnp.mean(wide, axis=-1, keepdims=True)
    centred = wide - average
    variance = jnp.mean(centred * centred, axis=-1, keepdims=True)
    return centred * lax.rsqrt(variance + 1e-06) * gain + shift


def attend(heads_qkv, token_segs):
    row_count = heads_qkv.shape[0]
    width = heads_qkv.shape[2] // 3
    queries = heads_qkv[:, :, :width]
    keys_all = heads_qkv[:, :, width : 2 * width]
    values_all = heads_qkv[:, :, 2 * width :]
    score_scale = 1.0 / jnp.sqrt(jnp.float32(width))
    block_rows = min(512, row_count)
    outputs = []
    for block_index in range(row_count // block_rows):
        lower = block_index * block_rows
        scores = (
            jnp.einsum(
                "qhd,khd->hqk",
                queries[lower : lower + block_rows],
                keys_all,
                preferred_element_type=jnp.float32,
            )
            * score_scale
        )
        same = token_segs[lower : lower + block_rows][:, None] == token_segs[None, :]
        scores = jnp.where(same[None], scores, -jnp.inf)
        row_max = jnp.max(scores, axis=-1, keepdims=True)
        exponent = jnp.exp(scores - row_max)
        probs = (exponent / jnp.sum(exponent, axis=-1, keepdims=True)).astype(jnp.bfloat16)
        context = jnp.einsum("hqk,khd->qhd", probs, values_all, preferred_element_type=jnp.float32)
        outputs.append(context.astype(jnp.bfloat16))
    return jnp.concatenate(outputs, axis=0)


def shards(
    tokens,
    ln1_gain,
    ln1_shift,
    w_qkv,
    w_out,
    ln2_gain,
    ln2_shift,
    w_proj,
    proj_bias,
    segments,
    owners,
):
    dp_count = lax.axis_size("dp")
    gathered = lax.all_gather(tokens, "tensor", axis=0, tiled=True)
    row_count = gathered.shape[0]
    normed = layer_norm(gathered, ln1_gain, ln1_shift).astype(jnp.bfloat16)
    heads_here = w_qkv.shape[1]
    heads_qkv = jnp.dot(
        normed, w_qkv.reshape(w_qkv.shape[0], -1), preferred_element_type=jnp.float32
    )
    heads_qkv = heads_qkv.astype(jnp.bfloat16).reshape(row_count, heads_here, -1)
    token_segs = jnp.repeat(segments[0], 4)
    context = attend(heads_qkv, token_segs).reshape(row_count, -1)
    out_flat = w_out.reshape(-1, w_out.shape[2])
    attn_all = lax.psum(
        jnp.dot(context, out_flat, preferred_element_type=jnp.float32).astype(jnp.bfloat16),
        "tensor",
    ).astype(jnp.float32)
    hidden = (gathered.astype(jnp.float32) + attn_all).astype(jnp.bfloat16)
    normed_all = layer_norm(hidden, ln2_gain, ln2_shift).astype(jnp.bfloat16)
    groups = row_count // 4
    merged = normed_all.reshape(groups, -1)
    summed = jnp.dot(
        merged, lax.all_gather(w_proj, "dp", axis=0, tiled=True), preferred_element_type=jnp.float32
    )
    projected = (summed + proj_bias).astype(jnp.bfloat16)
    dests = owners[:, 0]
    onehot = (dests[:, None] == jnp.arange(dp_count, dtype=jnp.int32)[None, :]).astype(jnp.int32)
    earlier = jnp.cumsum(onehot, axis=0) - onehot
    position = jnp.sum(earlier * onehot, axis=1)
    capacity = 2 * groups // dp_count
    slot_index = dests * capacity + position
    scatter_table = (
        slot_index[None, :] == jnp.arange(dp_count * capacity, dtype=jnp.int32)[:, None]
    ).astype(jnp.bfloat16)
    outgoing = jnp.dot(scatter_table, projected, preferred_element_type=jnp.float32).astype(
        jnp.bfloat16
    )
    outgoing = outgoing.reshape(dp_count, capacity, -1)
    arrived = lax.all_to_all(outgoing, "dp", split_axis=0, concat_axis=0, tiled=True)
    return arrived.reshape(dp_count * capacity, -1)


def norm_rows(wide, gain, shift):
    average = jnp.mean(wide, axis=-1, keepdims=True)
    centred = wide - average
    variance = jnp.mean(centred * centred, axis=-1, keepdims=True)
    return centred * lax.rsqrt(variance + 1e-06) * gain + shift


MESH = pl.DeviceIdType.MESH
FIRST_SENDS = ((0, 4), (0, 1), (0, 2), (0, 8))
AFTER_PAIR = ((4, 8), (4, 2), (4, 1))
DELIVERY = (12, 8, 13, 9, 14, 10, 15, 11, 4, 5, 6, 7, 1, 2, 3)
ALL_SENDS = FIRST_SENDS + AFTER_PAIR + ((1, 2), (8, 1), (8, 2), (6, 1), (12, 2), (12, 1), (9, 2), (14, 1))


def flipped(index, offset):
    result = index
    for bit in range(4):
        if offset >> bit & 1:
            result = result + (1 << bit) * (1 - 2 * (index // (1 << bit) % 2))
    return result


def as_row(ref):
    return jnp.concatenate([ref[i : i + 1, :] for i in range(ref.shape[0])], axis=1)


def slot_row(owner_row, owners_count, capacity):
    groups = owner_row.shape[1]
    numbers = lax.broadcasted_iota(jnp.int32, (owners_count, groups), 0)
    onehot = numbers == owner_row
    rows = lax.broadcasted_iota(jnp.int32, (groups, groups), 0)
    lanes = lax.broadcasted_iota(jnp.int32, (groups, groups), 1)
    before = (rows < lanes).astype(jnp.bfloat16)
    earlier = jnp.dot(onehot.astype(jnp.bfloat16), before, preferred_element_type=jnp.float32)
    position = jnp.sum(jnp.where(onehot, earlier, 0.0), axis=0, keepdims=True)
    return owner_row * capacity + position.astype(jnp.int32)


def sublayer_kernel(
    own_ref,
    gain1_ref,
    shift1_ref,
    w_hbm_ref,
    segments_ref,
    w_out_hbm_ref,
    gain2_ref,
    shift2_ref,
    w_proj_ref,
    bias_ref,
    owners_ref,
    out_ref,
    w_ref,
    w_out_ref,
    peer_ref,
    normed_ref,
    context_ref,
    here_ref,
    there_ref,
    arrived_ref,
    pieces_ref,
    blocks_ref,
    gathered_ref,
    total_ref,
    outgoing_ref,
    far_owners_ref,
    segs_col_ref,
    segs_row_ref,
    send_sems,
    recv_sems,
    local_sems,
    give_sems,
    take_sems,
):
    dp, core = lax.axis_index("dp"), lax.axis_index("tensor")
    half, depth = own_ref.shape
    rows = 2 * half
    width = w_ref.shape[1] // 3
    columns = gathered_ref.shape[2]
    dp_count, _, capacity, _ = outgoing_ref.shape
    score_scale = 1.0 / math.sqrt(width)
    parity = dp // 4 % 2
    beside = (dp, 1 - core)
    facing = (flipped(dp, 4), core)

    def remote(source, target, number, device):
        return pltpu.make_async_remote_copy(
            src_ref=source,
            dst_ref=target,
            send_sem=send_sems.at[number],
            recv_sem=recv_sems.at[number],
            device_id=device,
            device_id_type=MESH,
        )

    def lanes_of(side):
        return pl.ds(pl.multiple_of(side * columns, 128), columns)

    def shard_copy(shard, partner):
        index = flipped(dp, shard)
        if shard == 0:
            side = 1 - parity if partner == 4 else parity
            source = w_proj_ref.at[:, lanes_of(side)]
        else:
            source = gathered_ref.at[index]
        return remote(source, gathered_ref.at[index], shard ^ partner, (flipped(dp, partner), core))

    def wait_shard(offset):
        place = gathered_ref.at[flipped(dp, offset)]
        remote(place, place, offset, facing).wait_recv()

    def deliver(offset, pack):
        source = flipped(dp, 4 * pack)
        rows_at = pl.ds(pl.multiple_of(source * capacity, capacity), capacity)
        owner = flipped(dp, offset)
        target = out_ref.at[rows_at, lanes_of(parity)]
        if offset == 0:
            return pltpu.make_async_copy(outgoing_ref.at[dp, pack], target, take_sems.at[0, pack])
        return pltpu.make_async_remote_copy(
            src_ref=outgoing_ref.at[owner, pack],
            dst_ref=target,
            send_sem=give_sems.at[offset, pack],
            recv_sem=take_sems.at[offset, pack],
            device_id=(owner, core),
            device_id_type=MESH,
        )

    def wait_delivery(offset, pack):
        sender = flipped(dp, offset)
        source = flipped(sender, 4 * pack)
        rows_at = pl.ds(pl.multiple_of(source * capacity, capacity), capacity)
        target = out_ref.at[rows_at, lanes_of(sender // 4 % 2)]
        pltpu.make_async_remote_copy(
            src_ref=target,
            dst_ref=target,
            send_sem=give_sems.at[offset, pack],
            recv_sem=take_sems.at[offset, pack],
            device_id=(sender, core),
            device_id_type=MESH,
        ).wait_recv()

    barrier = pltpu.get_barrier_semaphore()
    for device in [(flipped(dp, offset), core) for offset in range(1, dp_count)] + [beside]:
        pl.semaphore_signal(barrier, inc=1, device_id=device, device_id_type=MESH)
    pl.semaphore_wait(barrier, dp_count)

    token_copy = remote(own_ref, peer_ref, 16, beside)
    token_copy.start()
    for send in FIRST_SENDS:
        shard_copy(*send).start()
    owners_copy = remote(owners_ref, far_owners_ref, 21, facing)
    owners_copy.start()
    w_copy = pltpu.make_async_copy(w_hbm_ref, w_ref, local_sems.at[0])
    w_copy.start()
    w_out_copy = pltpu.make_async_copy(w_out_hbm_ref, w_out_ref, local_sems.at[1])
    w_out_copy.start()
    own_copy = pltpu.make_async_copy(
        w_proj_ref.at[:, lanes_of(parity)], gathered_ref.at[dp], local_sems.at[2]
    )
    own_copy.start()

    groups = segments_ref.shape[1]
    spread = (
        lax.broadcasted_iota(jnp.int32, (groups, rows), 0)
        == lax.shift_right_logical(lax.broadcasted_iota(jnp.int32, (groups, rows), 1), 2)
    ).astype(jnp.bfloat16)
    images = jnp.broadcast_to(segments_ref[...].astype(jnp.float32), (128, groups))
    token_images = jnp.dot(
        images.astype(jnp.bfloat16), spread, preferred_element_type=jnp.float32
    )
    segs_row_ref[...] = token_images[:1]
    segs_col_ref[...] = token_images.T[:, :1]

    step_rows = 128

    def first_norm(part, source):
        gain, shift = as_row(gain1_ref), as_row(shift1_ref)

        @pl.loop(0, half // step_rows)
        def _(step):
            at = pl.multiple_of(step * step_rows, step_rows)
            wide = source[pl.ds(at, step_rows), :].astype(jnp.float32)
            to = pl.multiple_of(part * half + step * step_rows, step_rows)
            normed = norm_rows(wide, gain, shift)
            normed_ref[pl.ds(to, step_rows), :] = normed.astype(jnp.bfloat16)

    first_norm(core, own_ref)
    token_copy.wait_recv()
    first_norm(1 - core, peer_ref)
    w_copy.wait()

    chunk = 256

    def heads(first, last):
        @pl.loop(first, last)
        def _(head):
            qkv = lax.dot_general(
                w_ref[head],
                normed_ref[...],
                (((1,), (1,)), ((), ())),
                preferred_element_type=jnp.float32,
            )
            queries = qkv[:width].astype(jnp.bfloat16)
            keys = qkv[width : 2 * width].T.astype(jnp.bfloat16)
            values = qkv[2 * width :].astype(jnp.bfloat16)
            for index in range(rows // chunk):
                lanes = slice(index * chunk, (index + 1) * chunk)
                scores = jnp.dot(keys, queries[:, lanes], preferred_element_type=jnp.float32)
                same = segs_col_ref[...] == segs_row_ref[:, lanes]
                scores = jnp.where(same, scores * score_scale, -jnp.inf)
                exponent = jnp.exp(scores - jnp.max(scores, axis=0, keepdims=True))
                total = jnp.sum(exponent, axis=0, keepdims=True)
                summed = jnp.dot(
                    values, exponent.astype(jnp.bfloat16), preferred_element_type=jnp.float32
                )
                context_ref[head, :, lanes] = summed / total

    heads(0, 3)
    wait_shard(4)
    for send in AFTER_PAIR:
        shard_copy(*send).start()
    heads(3, 6)
    wait_shard(1)
    shard_copy(1, 2).start()
    heads(6, 7)
    wait_shard(6)
    shard_copy(6, 1).start()
    heads(7, w_ref.shape[0])

    def terms(side, target):
        for index in range(half // chunk):
            lanes = pl.ds(pl.multiple_of(side * half + index * chunk, chunk), chunk)
            context = context_ref[:, :, lanes].reshape(-1, chunk).T.astype(jnp.bfloat16)
            term = jnp.dot(context, w_out_ref[...], preferred_element_type=jnp.float32)
            target[index * chunk : (index + 1) * chunk, :] = term.astype(jnp.bfloat16)

    w_out_copy.wait()
    terms(1 - core, there_ref)
    term_copy = remote(there_ref, arrived_ref, 17, beside)
    term_copy.start()
    wait_shard(8)
    shard_copy(8, 1).start()
    shard_copy(8, 2).start()
    terms(core, here_ref)
    term_copy.wait_recv()
    gain2, shift2 = as_row(gain2_ref), as_row(shift2_ref)

    @pl.loop(0, half // step_rows)
    def _(step):
        at = pl.ds(pl.multiple_of(step * step_rows, step_rows), step_rows)
        attn = here_ref[at, :].astype(jnp.float32) + arrived_ref[at, :].astype(jnp.float32)
        hidden = (own_ref[at, :].astype(jnp.float32) + attn).astype(jnp.bfloat16)
        normed = norm_rows(hidden.astype(jnp.float32), gain2, shift2)
        for piece in range(depth // 128):
            pieces_ref[piece] = normed[:, piece * 128 : (piece + 1) * 128]
        quarter = step_rows // 4
        to = pl.ds(pl.multiple_of(step * quarter, quarter), quarter)
        for place in range(4):
            for piece in range(depth // 128):
                picked = pieces_ref[piece, pl.ds(place, quarter, stride=4), :]
                lanes = slice(piece * 128, (piece + 1) * 128)
                blocks_ref[0, place, to, lanes] = picked.astype(jnp.bfloat16)

    far_copy = remote(blocks_ref.at[0], blocks_ref.at[2], 18, facing)
    far_copy.start()
    near_copy = remote(blocks_ref.at[0], blocks_ref.at[1], 19, beside)
    near_copy.start()

    block_rows = blocks_ref.shape[2]

    def project(offset, first, fresh):
        place = flipped(dp, offset) // 4
        weights = gathered_ref[pl.ds(4 * place, 4)].reshape(-1, columns)
        for block in (first, first + 1):
            part = core if block == first else 1 - core
            at = pl.ds(pl.multiple_of((first + part) * block_rows, block_rows), block_rows)
            product = jnp.dot(blocks_ref[block, place], weights, preferred_element_type=jnp.float32)
            total_ref[at, :] = product if fresh else total_ref[at, :] + product

    biases = as_row(bias_ref)
    bias = jnp.where(parity == 0, biases[:, :columns], biases[:, columns:])
    places = lax.broadcasted_iota(jnp.int32, (dp_count * capacity, groups), 0)

    def send_pack(pack, owner_row):
        at = slice(2 * pack * block_rows, 2 * (pack + 1) * block_rows)
        projected = (total_ref[at, :] + bias).astype(jnp.bfloat16)
        table = (places == slot_row(owner_row, dp_count, capacity)).astype(jnp.bfloat16)
        placed = jnp.dot(table, projected, preferred_element_type=jnp.float32)
        outgoing_ref[:, pack] = placed.astype(jnp.bfloat16).reshape(dp_count, capacity, columns)
        for offset in DELIVERY + (0,):
            deliver(offset, pack).start()

    wait_shard(12)
    shard_copy(12, 2).start()
    shard_copy(12, 1).start()
    wait_shard(9)
    shard_copy(9, 2).start()
    near_copy.wait_recv()
    own_copy.wait()
    wait_shard(2)
    wait_shard(3)
    project(0, 0, True)
    wait_shard(14)
    shard_copy(14, 1).start()
    far_copy.wait_recv()
    across_copy = remote(blocks_ref.at[2], blocks_ref.at[3], 20, beside)
    across_copy.start()
    wait_shard(5)
    wait_shard(7)
    project(4, 0, False)
    across_copy.wait_recv()
    project(0, 2, True)
    project(4, 2, False)
    wait_shard(10)
    wait_shard(11)
    project(8, 0, False)
    project(8, 2, False)
    wait_shard(13)
    wait_shard(15)
    project(12, 0, False)
    send_pack(0, owners_ref[...])
    project(12, 2, False)
    owners_copy.wait_recv()
    send_pack(1, far_owners_ref[...])

    for send in ALL_SENDS:
        shard_copy(*send).wait_send()
    for copy in (token_copy, owners_copy, term_copy, far_copy, near_copy, across_copy):
        copy.wait_send()
    for pack in range(2):
        deliver(0, pack).wait()
        for offset in DELIVERY:
            wait_delivery(offset, pack)
            deliver(offset, pack).wait_send()


def paired_shards(
    tokens,
    ln1_gain,
    ln1_shift,
    w_qkv,
    w_out,
    ln2_gain,
    ln2_shift,
    w_proj,
    proj_bias,
    segments,
    owners,
):
    dp_count = lax.axis_size("dp")
    columns = w_proj.shape[1] // 2
    half, depth = tokens.shape
    groups = 2 * half // 4
    capacity = 2 * groups // dp_count
    heads_here, width, _ = w_out.shape
    w_heads = w_qkv.transpose(1, 2, 0)
    w_out_rows = w_out.reshape(-1, depth)
    half_rows = pltpu.VMEM((half, depth), jnp.bfloat16)
    near = pl.BlockSpec(memory_space=pltpu.VMEM)
    away = pl.BlockSpec(memory_space=pl.ANY)
    return pl.pallas_call(
        sublayer_kernel,
        in_specs=[near, near, near, away, near, away, near, near, away, near, near],
        out_specs=near,
        out_shape=jax.ShapeDtypeStruct((dp_count * capacity, 2 * columns), jnp.bfloat16),
        scratch_shapes=[
            pltpu.VMEM(w_heads.shape, jnp.bfloat16),
            pltpu.VMEM(w_out_rows.shape, jnp.bfloat16),
            half_rows,
            pltpu.VMEM((2 * half, depth), jnp.bfloat16),
            pltpu.VMEM((heads_here, width, 2 * half), jnp.float32),
            half_rows,
            half_rows,
            half_rows,
            pltpu.VMEM((depth // 128, 128, 128), jnp.float32),
            pltpu.VMEM((4, 4, half // 4, depth), jnp.bfloat16),
            pltpu.VMEM((dp_count, w_proj.shape[0], columns), jnp.bfloat16),
            pltpu.VMEM((half, columns), jnp.float32),
            pltpu.VMEM((dp_count, 2, capacity, columns), jnp.bfloat16),
            pltpu.VMEM((1, groups), jnp.int32),
            pltpu.VMEM((2 * half, 1), jnp.float32),
            pltpu.VMEM((1, 2 * half), jnp.float32),
            pltpu.SemaphoreType.DMA((22,)),
            pltpu.SemaphoreType.DMA((22,)),
            pltpu.SemaphoreType.DMA((3,)),
            pltpu.SemaphoreType.DMA((dp_count, 2)),
            pltpu.SemaphoreType.DMA((dp_count, 2)),
        ],
        compiler_params=pltpu.CompilerParams(
            collective_id=0, has_side_effects=True, vmem_limit_bytes=60 * 2**20
        ),
        cost_estimate=pl.CostEstimate(flops=10**10, bytes_accessed=10**7, transcendentals=0),
    )(
        tokens,
        ln1_gain.reshape(-1, 128),
        ln1_shift.reshape(-1, 128),
        w_heads,
        segments,
        w_out_rows,
        ln2_gain.reshape(-1, 128),
        ln2_shift.reshape(-1, 128),
        w_proj,
        proj_bias.reshape(-1, 128),
        owners.reshape(1, groups),
    )


def solution(mesh):
    paired = mesh.shape["tensor"] == 2 and mesh.shape["dp"] == 16
    return jax.shard_map(
        paired_shards if paired else shards,
        mesh=mesh,
        in_specs=(
            P(("dp", "tensor"), None),
            P(),
            P(),
            P(None, "tensor", None),
            P("tensor", None, None),
            P(),
            P(),
            P("dp", "tensor"),
            P("tensor"),
            P("dp", None),
            P("dp", None),
        ),
        out_specs=P("dp", "tensor"),
        check_vma=False,
    )
```
